256 devices in a mesh: row: 8 (over x_hi, y), col: 32 (over z, x_lo, core).
Axes of the slice: x: 4 (x_hi: 2, x_lo: 2; x = x_hi * 2 + x_lo), y: 4, z: 8, core: 2. Of those that a mesh axis runs over, the one named last changes fastest.
Arguments:
- layer_inputs: bfloat16 [1024, 4608], P('col', 'row'), may hold values from -6 to 6
- cotangent: bfloat16 [1024, 4608], P('col', 'row'), may hold values from -1.5 to 1.5
- gate_saved: bfloat16 [1024, 36864], P('row', 'col'), may hold values from -6 to 6
- up_saved: bfloat16 [1024, 36864], P('row', 'col'), may hold values from -6 to 6
- gate_weight: bfloat16 [4608, 36864], P('row', 'col'), may hold values from -0.09375 to 0.09375
- up_weight: bfloat16 [4608, 36864], P('row', 'col'), may hold values from -0.09375 to 0.09375
- down_weight: bfloat16 [36864, 4608], P('col', 'row'), may hold values from -0.03125 to 0.03125
Outputs:
- input_grad: bfloat16 [1024, 4608], P('col', 'row')
- gate_weight_grad: bfloat16 [4608, 36864], P('row', 'col')
- up_weight_grad: bfloat16 [4608, 36864], P('row', 'col')
- down_weight_grad: bfloat16 [36864, 4608], P('col', 'row')
The draws below stay inside these ranges and needn't reach their ends.
All inputs are finite; a program needn't handle non-finite values.
Results may differ from the reference program's by a relative error of at most 0.005.
Values may be sent and summed in bfloat16 or wider, within the bound.
A program may use at most 64 MiB of HBM per device.

```python
import jax
import jax.numpy as jnp
from jax import lax

D = 4608
FF = 36864
TOKENS = 1024


def with_spikes(result, rng, source, target, parts, factor):
    owner, partner = [(jnp.arange(result.shape[dim]) // (result.shape[dim] // parts)).reshape([-1 if axis == dim else 1 for axis in range(result.ndim)]) for dim in (source, target)]
    chosen = jax.random.permutation(rng, parts)[partner]
    strong = (owner == chosen) | (owner == (partner + parts // 2) % parts)
    return jnp.where(strong, factor * result, result)


def steps_of(rng, extent, pieces, smallest, high):
    loudness, own = 1.0, jax.random.fold_in(rng, 6)
    for axis_at, parts in pieces:
        steps = jnp.exp(jax.random.uniform(jax.random.fold_in(own, axis_at), (parts,), jnp.float32, smallest / len(pieces), high / len(pieces)))
        loudness = loudness * jnp.repeat(steps, extent[axis_at] // parts).reshape([-1 if axis == axis_at else 1 for axis in range(len(extent))])
    return loudness


def normal_values(stream_key, dims, deviation, limit, pieces=(), held_as=jnp.bfloat16):
    factor_of = steps_of(stream_key, dims, pieces, -0.22, 0.18) if pieces else 1.0
    drawn = jax.random.normal(stream_key, dims, jnp.float32) * deviation * factor_of
    return jnp.minimum(jnp.maximum(drawn, -limit), limit).astype(held_as)


def noise_with(stream_key, shape, scale, reach, split, heavy, kind=jnp.bfloat16):
    array = scale * jax.random.normal(stream_key, shape, jnp.float32)
    if split:
        array = array * steps_of(stream_key, shape, split, -0.22, 0.18)
    return jnp.clip(with_spikes(array, jax.random.fold_in(stream_key, 3), *heavy), -reach, reach).astype(kind)


def setup_inputs(seed: int = 0) -> dict:
    keys = jax.random.split(jax.random.key(seed), 8)
    layer_inputs = normal_values(keys[0], (TOKENS, D), 1.0, 6.0, ((0, 32), (1, 8)))
    cotangent = noise_with(keys[1], (TOKENS, D), 0.25, 1.5, ((0, 32), (1, 8)), (1, 0, 32, 2.75))
    gate_saved = normal_values(keys[2], (TOKENS, FF), 1.0, 6.0, ((0, 8), (1, 32)))
    up_saved = normal_values(keys[3], (TOKENS, FF), 1.0, 6.0, ((0, 8), (1, 32)))
    gate_weight = normal_values(keys[4], (D, FF), D ** -0.5, 0.09375, ((0, 8), (1, 32)))
    up_weight = normal_values(keys[5], (D, FF), D ** -0.5, 0.09375, ((0, 8), (1, 32)))
    down_weight = normal_values(keys[6], (FF, D), FF ** -0.5, 0.03125, ((0, 32), (1, 8)))
    return dict(layer_inputs=layer_inputs, cotangent=cotangent, gate_saved=gate_saved, up_saved=up_saved, gate_weight=gate_weight, up_weight=up_weight, down_weight=down_weight)


SCALE_INNER = 0.7978845608028654
CUBIC_COEF = 0.044715


def gelu_parts(gate_value):
    inner_term = SCALE_INNER * (gate_value + CUBIC_COEF * gate_value * gate_value * gate_value)
    tangent = jnp.tanh(inner_term)
    gelu_value = 0.5 * gate_value * (1.0 + tangent)
    gelu_slope = 0.5 * (1.0 + tangent) + 0.5 * gate_value * (1.0 - tangent * tangent) * SCALE_INNER * (1.0 + 3.0 * CUBIC_COEF * gate_value * gate_value)
    return gelu_value, gelu_slope


def contract_first(first_operand, second_operand):
    return lax.dot_general(first_operand, second_operand, (((0,), (0,)), ((), ())), preferred_element_type=jnp.float32)


def contract_last(first_operand, second_operand):
    return lax.dot_general(first_operand, second_operand, (((1,), (1,)), ((), ())), preferred_element_type=jnp.float32)


def reference(layer_inputs, cotangent, gate_saved, up_saved, gate_weight, up_weight, down_weight):
    gate_value = gate_saved.astype(jnp.float32)
    up_value = up_saved.astype(jnp.float32)
    gelu_value, gelu_slope = gelu_parts(gate_value)
    hidden = (gelu_value * up_value).astype(jnp.bfloat16)
    hidden_grad = contract_last(cotangent, down_weight)
    gate_grad = (hidden_grad * up_value * gelu_slope).astype(jnp.bfloat16)
    up_grad = (hidden_grad * gelu_value).astype(jnp.bfloat16)
    down_weight_grad = contract_first(hidden, cotangent).astype(jnp.bfloat16)
    gate_weight_grad = contract_first(layer_inputs, gate_grad).astype(jnp.bfloat16)
    up_weight_grad = contract_first(layer_inputs, up_grad).astype(jnp.bfloat16)
    input_grad = (contract_last(gate_grad, gate_weight) + contract_last(up_grad, up_weight)).astype(jnp.bfloat16)
    return (input_grad, gate_weight_grad, up_weight_grad, down_weight_grad)
```

```python
import functools

import jax
import jax.numpy as jnp
from jax import lax
from jax.experimental import pallas as pl
from jax.experimental.pallas import tpu as pltpu
from jax.sharding import PartitionSpec as P

SCALE_INNER = 0.7978845608028654
CUBIC_COEF = 0.044715
MESH = pl.DeviceIdType.MESH
BF16 = jnp.bfloat16
F32 = jnp.float32

W = 576
U = 1152
NT = 384
N_REMOTE = 112


def gelu_parts(gate_value):
    inner_term = SCALE_INNER * (gate_value + CUBIC_COEF * gate_value * gate_value * gate_value)
    tangent = jnp.tanh(inner_term)
    gelu_value = 0.5 * gate_value * (1.0 + tangent)
    gelu_slope = 0.5 * (1.0 + tangent) + 0.5 * gate_value * (
        1.0 - tangent * tangent
    ) * SCALE_INNER * (1.0 + 3.0 * CUBIC_COEF * gate_value * gate_value)
    return (gelu_value, gelu_slope)


def dot_nt(a, b):
    return lax.dot_general(a, b, (((1,), (1,)), ((), ())), preferred_element_type=F32)


def dot_tn(a, b):
    return lax.dot_general(a, b, (((0,), (0,)), ((), ())), preferred_element_type=F32)


def kernel(
    inp_h, cot_h, g_h, u_h, gw_h, uw_h, dw_h,
    ig_o, gwg_o, uwg_o, dwg_o,
    cot_all, inp_all, h_all, gg_all, ug_all, part,
    g_v, u_v, dw_v, gw_v, uw_v, val, slope_up,
    ry_relay, ry_full, sy, sx, rx, q_own,
    ig_part, ig_core, ig_send, ig_recv, ig_red, ig_fin, ig_out,
    gwg_v, uwg_v, dwg_v,
    lsem, ssem, rsem,
):
    row, col = lax.axis_index("row"), lax.axis_index("col")
    xh, y = lax.div(row, 4), lax.rem(row, 4)
    z, xl, co = lax.div(col, 4), lax.rem(lax.div(col, 2), 2), lax.rem(col, 2)
    y_next, y_prev, y_far = lax.rem(y + 1, 4), lax.rem(y + 3, 4), lax.rem(y + 2, 4)
    zs = [lax.rem(z + k, 8) for k in range(8)]

    yp = (xh * 4 + y_next, col)
    ym = (xh * 4 + y_prev, col)
    x2 = ((1 - xh) * 4 + y, col)
    mate = (row, col + 1 - 2 * co)
    side = (row, z * 4 + (1 - xl) * 2 + co)
    zd = [None] + [(row, zs[k] * 4 + xl * 2 + co) for k in range(1, 8)]
    partners = [yp, ym, x2, mate, side] + zd[1:]

    def load(i, src, dst):
        cp = pltpu.make_async_copy(src, dst, lsem.at[i])
        cp.start()
        return cp

    l_cot = load(0, cot_h, cot_all.at[z, xl, co])
    l_g = load(1, g_h, g_v)
    l_u = load(2, u_h, u_v)
    l_inp = load(3, inp_h, inp_all.at[z, xl, co])
    l_dw = load(4, dw_h, dw_v)
    l_gw = load(5, gw_h, gw_v)
    l_uw = load(6, uw_h, uw_v)

    barrier = pltpu.get_barrier_semaphore()
    for d in partners:
        pl.semaphore_signal(barrier, inc=1, device_id=d, device_id_type=MESH)
    pl.semaphore_wait(barrier, len(partners))

    sends = []

    def send(src, dst, device):
        i = len(sends)
        cp = pltpu.make_async_remote_copy(
            src_ref=src, dst_ref=dst, send_sem=ssem.at[i], recv_sem=rsem.at[i],
            device_id=device, device_id_type=MESH,
        )
        cp.start()
        sends.append(cp)
        return cp

    def col_start(buf):
        return send(buf.at[z, xl, co], buf.at[z, xl, co], side)

    def col_pair(buf, k, device):
        return send(buf.at[zs[k], :, co], buf.at[zs[k], :, co], device)

    def col_steps(buf, first):
        first.wait_recv()
        up = col_pair(buf, 0, zd[1])
        down = col_pair(buf, 0, zd[7])
        cores = [col_pair(buf, 0, mate)]
        yield
        for s in (1, 2, 3):
            up.wait_recv()
            if s < 3:
                up = col_pair(buf, 8 - s, zd[1])
            else:
                up = send(buf.at[zs[5], 0, co], buf.at[zs[5], 0, co], zd[1])
            cores.append(col_pair(buf, 8 - s, mate))
            down.wait_recv()
            if s < 3:
                down = col_pair(buf, s, zd[7])
            else:
                down = send(buf.at[zs[3], 1, co], buf.at[zs[3], 1, co], zd[7])
            cores.append(col_pair(buf, s, mate))
            yield
        up.wait_recv()
        down.wait_recv()
        cores.append(col_pair(buf, 4, mate))
        yield
        for cp in cores:
            cp.wait_recv()
        yield

    l_cot.wait()
    cot_first = col_start(cot_all)

    l_g.wait()
    l_u.wait()

    def act(i, carry):
        rows = pl.ds(pl.multiple_of(i * 32, 32), 32)
        gate_value = g_v[rows].astype(F32)
        up_value = u_v[rows].astype(F32)
        gelu_value, gelu_slope = gelu_parts(gate_value)
        h_all[xh, y, rows] = (gelu_value * up_value).astype(BF16)
        val[rows] = gelu_value
        slope_up[rows] = up_value * gelu_slope
        return carry

    lax.fori_loop(0, 4, act, 0)

    h_up = send(h_all.at[xh, y], h_all.at[xh, y], yp)
    h_down = send(h_all.at[xh, y], h_all.at[xh, y], ym)
    h_x = [send(h_all.at[xh, y], h_all.at[xh, y], x2)]
    l_inp.wait()
    inp_first = col_start(inp_all)

    steps = col_steps(cot_all, cot_first)
    for _ in range(5):
        next(steps)

    A, B = pl.ds(0, 64), pl.ds(64, 64)
    h_up.wait_recv()
    h_ru = send(h_all.at[xh, y_prev, A], h_all.at[xh, y_prev, A], yp)
    h_x.append(send(h_all.at[xh, y_prev], h_all.at[xh, y_prev], x2))
    h_down.wait_recv()
    h_rd = send(h_all.at[xh, y_next, B], h_all.at[xh, y_next, B], ym)
    h_x.append(send(h_all.at[xh, y_next], h_all.at[xh, y_next], x2))

    next(steps)
    inp_steps = col_steps(inp_all, inp_first)

    l_dw.wait()

    def partial(h):
        def tile(n, carry):
            cols = pl.ds(pl.multiple_of(n * NT, 128), NT)
            lhs = cot_all[:, h].reshape(512, W)
            part[h, :, :, :, cols] = dot_nt(lhs, dw_v[cols]).astype(BF16).reshape(2, 4, 64, NT)
            return carry

        lax.fori_loop(0, U // NT, tile, 0)

    lo, hi = pl.ds(0, 32), pl.ds(32, 32)

    def rs_first(h):
        relay_up = send(part.at[h, :, y_far, lo], ry_relay.at[h, 0], yp)
        relay_down = send(part.at[h, :, y_far, hi], ry_relay.at[h, 1], ym)
        direct_up = send(part.at[h, :, y_next, hi], ry_full.at[h, 0, :, hi], yp)
        direct_down = send(part.at[h, :, y_prev, lo], ry_full.at[h, 1, :, lo], ym)
        return relay_up, relay_down, direct_up, direct_down

    def rs_second(h, relay_up, relay_down):
        relay_up.wait_recv()
        sy[h, 0] = (part[h, :, y_next, 0:32].astype(F32) + ry_relay[h, 0].astype(F32)).astype(BF16)
        both_up = send(sy.at[h, 0], ry_full.at[h, 0, :, lo], yp)
        relay_down.wait_recv()
        sy[h, 1] = (part[h, :, y_prev, 32:64].astype(F32) + ry_relay[h, 1].astype(F32)).astype(BF16)
        both_down = send(sy.at[h, 1], ry_full.at[h, 1, :, hi], ym)
        return both_up, both_down

    def rs_third(h, waits):
        for cp in waits:
            cp.wait_recv()

        def total(which):
            return (
                part[h, which, y].astype(F32)
                + ry_full[h, 0, which].astype(F32)
                + ry_full[h, 1, which].astype(F32)
            )

        sx[h] = total(1 - xh).astype(BF16)
        cp = send(sx.at[h], rx.at[h], x2)
        q_own[h] = total(xh)
        return cp

    def grads(h, cp):
        cp.wait_recv()
        hidden_grad = q_own[h] + rx[h].astype(F32)
        gg_all[h, xh, y] = (hidden_grad * slope_up[h * 64 : h * 64 + 64]).astype(BF16)
        ug_all[h, xh, y] = (hidden_grad * val[h * 64 : h * 64 + 64]).astype(BF16)

    def ag(ref, h, k, yy, device, rows=None):
        r = ref.at[h, k, yy] if rows is None else ref.at[h, k, yy, rows]
        return send(r, r, device)

    class Gather:
        def start(self, h):
            self.h = h
            self.gx = ag(gg_all, h, xh, y, x2)
            self.gu = [ag(gg_all, h, xh, y, yp)]
            self.gd = [ag(gg_all, h, xh, y, ym)]
            self.uu = ag(ug_all, h, xh, y, yp)
            self.ud = ag(ug_all, h, xh, y, ym)
            self.ux = [ag(ug_all, h, xh, y, x2)]

        def across(self):
            h = self.h
            self.gx.wait_recv()
            self.gu.append(ag(gg_all, h, 1 - xh, y, yp))
            self.gd.append(ag(gg_all, h, 1 - xh, y, ym))

        def relay(self):
            h = self.h
            self.rest = []
            self.gu[0].wait_recv()
            self.rest.append(ag(gg_all, h, xh, y_prev, yp, lo))
            self.gd[0].wait_recv()
            self.rest.append(ag(gg_all, h, xh, y_next, ym, hi))
            self.uu.wait_recv()
            self.ru = ag(ug_all, h, xh, y_prev, yp, lo)
            self.ux.append(ag(ug_all, h, xh, y_prev, x2))
            self.ud.wait_recv()
            self.rd = ag(ug_all, h, xh, y_next, ym, hi)
            self.ux.append(ag(ug_all, h, xh, y_next, x2))
            self.gu[1].wait_recv()
            self.rest.append(ag(gg_all, h, 1 - xh, y_prev, yp, lo))
            self.gd[1].wait_recv()
            self.rest.append(ag(gg_all, h, 1 - xh, y_next, ym, hi))

        def last(self):
            self.ru.wait_recv()
            self.rd.wait_recv()
            self.ux.append(ag(ug_all, self.h, xh, y_far, x2))

        def done(self):
            for cp in self.rest + self.ux:
                cp.wait_recv()

    def input_grad(h):
        total = dot_nt(gg_all[h].reshape(512, U), gw_v[...])
        total += dot_nt(ug_all[h].reshape(512, U), uw_v[...])
        ig_part[h] = total.reshape(8, 2, 32, W)
        return send(ig_part.at[h, :, 1 - co], ig_core.at[h], mate)

    def input_grad_send(h, cp):
        cp.wait_recv()
        ig_send[h] = (ig_part[h, :, co] + ig_core[h]).astype(BF16)
        return [send(ig_send.at[h, zs[k]], ig_recv.at[h, k - 1], zd[k]) for k in range(1, 8)]

    def input_grad_sum(h, cps):
        total = ig_part[h, z, co] + ig_core[h, z]
        for cp in cps:
            cp.wait_recv()
        for k in range(7):
            total += ig_recv[h, k].astype(F32)
        ig_red[h] = total

    def weight_grad(grad_all, out):
        def tile(n, carry):
            cols = pl.ds(pl.multiple_of(n * NT, 128), NT)
            total = dot_tn(inp_all[:, 0].reshape(512, W), grad_all[0, :, :, :, cols].reshape(512, NT))
            total += dot_tn(inp_all[:, 1].reshape(512, W), grad_all[1, :, :, :, cols].reshape(512, NT))
            out[:, cols] = total.astype(BF16)
            return carry

        lax.fori_loop(0, U // NT, tile, 0)

    def down_grad():
        def tile(n, carry):
            cols = pl.ds(pl.multiple_of(n * NT, 128), NT)
            lhs = h_all[:, :, :, cols].reshape(1024, NT)
            dwg_v[cols] = dot_tn(lhs, cot_all[...].reshape(1024, W)).astype(BF16)
            return carry

        lax.fori_loop(0, U // NT, tile, 0)

    partial(0)
    ru0, rd0, du0, dd0 = rs_first(0)
    next(inp_steps)
    partial(1)
    next(inp_steps)
    bu0, bd0 = rs_second(0, ru0, rd0)
    ru1, rd1, du1, dd1 = rs_first(1)
    h_ru.wait_recv()
    h_rd.wait_recv()
    h_x.append(send(h_all.at[xh, y_far], h_all.at[xh, y_far], x2))
    next(inp_steps)
    x0 = rs_third(0, (du0, dd0, bu0, bd0))
    bu1, bd1 = rs_second(1, ru1, rd1)
    for _ in range(3):
        next(inp_steps)
    grads(0, x0)
    g0, g1 = Gather(), Gather()
    g0.start(0)
    x1 = rs_third(1, (du1, dd1, bu1, bd1))
    g0.across()
    grads(1, x1)
    for cp in h_x:
        cp.wait_recv()
    down_grad()
    outs = [load(7, dwg_v, dwg_o)]
    g0.relay()
    g1.start(1)
    g0.last()
    g1.across()
    l_gw.wait()
    l_uw.wait()
    g0.done()
    c0 = input_grad(0)
    g1.relay()
    z0 = input_grad_send(0, c0)
    g1.last()
    input_grad_sum(0, z0)
    g1.done()
    c1 = input_grad(1)
    z1 = input_grad_send(1, c1)
    weight_grad(gg_all, gwg_v)
    outs.append(load(8, gwg_v, gwg_o))
    weight_grad(ug_all, uwg_v)
    outs.append(load(9, uwg_v, uwg_o))
    input_grad_sum(1, z1)
    fin = send(ig_red.at[1 - xl], ig_fin, side)
    fin.wait_recv()
    ig_out[...] = (ig_red[xl] + ig_fin[...]).astype(BF16)
    outs.append(load(10, ig_out, ig_o))
    for cp in sends:
        cp.wait_send()
    for cp in outs:
        cp.wait()


def body(layer_inputs, cotangent, gate_saved, up_saved, gate_weight, up_weight, down_weight):
    any_spec = pl.BlockSpec(memory_space=pl.ANY)

    def bf(*shape):
        return pltpu.VMEM(shape, BF16)

    def f32(*shape):
        return pltpu.VMEM(shape, F32)

    return pl.pallas_call(
        kernel,
        out_shape=(
            jax.ShapeDtypeStruct((32, W), BF16),
            jax.ShapeDtypeStruct((W, U), BF16),
            jax.ShapeDtypeStruct((W, U), BF16),
            jax.ShapeDtypeStruct((U, W), BF16),
        ),
        in_specs=[any_spec] * 7,
        out_specs=[any_spec] * 4,
        scratch_shapes=[
            bf(8, 2, 2, 32, W), bf(8, 2, 2, 32, W), bf(2, 4, 128, U),
            bf(2, 2, 4, 64, U), bf(2, 2, 4, 64, U), bf(2, 2, 4, 64, U),
            bf(128, U), bf(128, U), bf(U, W), bf(W, U), bf(W, U), f32(128, U), f32(128, U),
            bf(2, 2, 2, 32, U), bf(2, 2, 2, 64, U), bf(2, 2, 2, 32, U), bf(2, 64, U), bf(2, 64, U), f32(2, 64, U),
            f32(2, 8, 2, 32, W), f32(2, 8, 32, W), bf(2, 8, 32, W), bf(2, 7, 32, W), f32(2, 32, W), f32(32, W), bf(32, W),
            bf(W, U), bf(W, U), bf(U, W),
            pltpu.SemaphoreType.DMA((11,)),
            pltpu.SemaphoreType.DMA((N_REMOTE,)),
            pltpu.SemaphoreType.DMA((N_REMOTE,)),
        ],
        compiler_params=pltpu.CompilerParams(
            collective_id=0, has_side_effects=True, vmem_limit_bytes=56 * 2**20
        ),
        cost_estimate=pl.CostEstimate(flops=8 * 10**9, bytes_accessed=9 * 10**6, transcendentals=150000),
    )(layer_inputs, cotangent, gate_saved, up_saved, gate_weight, up_weight, down_weight)


def solution(mesh):
    placed = (
        P("col", "row"),
        P("col", "row"),
        P("row", "col"),
        P("row", "col"),
        P("row", "col"),
        P("row", "col"),
        P("col", "row"),
    )
    return jax.shard_map(
        body,
        mesh=mesh,
        in_specs=placed,
        out_specs=(P("col", "row"), P("row", "col"), P("row", "col"), P("col", "row")),
        check_vma=False,
    )
```

```python
import functools

import jax
import jax.numpy as jnp
from jax import lax
from jax.experimental import pallas as pl
from jax.experimental.pallas import tpu as pltpu
from jax.sharding import PartitionSpec as P

SCALE_INNER = 0.7978845608028654
CUBIC_COEF = 0.044715
MESH = pl.DeviceIdType.MESH
BF16 = jnp.bfloat16
F32 = jnp.float32

W = 576
U = 1152
NT = 384
N_REMOTE = 140


def gelu_parts(gate_value):
    inner_term = SCALE_INNER * (gate_value + CUBIC_COEF * gate_value * gate_value * gate_value)
    tangent = jnp.tanh(inner_term)
    gelu_value = 0.5 * gate_value * (1.0 + tangent)
    gelu_slope = 0.5 * (1.0 + tangent) + 0.5 * gate_value * (
        1.0 - tangent * tangent
    ) * SCALE_INNER * (1.0 + 3.0 * CUBIC_COEF * gate_value * gate_value)
    return (gelu_value, gelu_slope)


def dot_nt(a, b):
    return lax.dot_general(a, b, (((1,), (1,)), ((), ())), preferred_element_type=F32)


def dot_nn(a, b):
    return lax.dot_general(a, b, (((1,), (0,)), ((), ())), preferred_element_type=F32)


def dot_tn(a, b):
    return lax.dot_general(a, b, (((0,), (0,)), ((), ())), preferred_element_type=F32)


def kernel(
    inp_h, cot_h, g_h, u_h, gw_h, uw_h, dw_h,
    ig_o, gwg_o, uwg_o, dwg_o,
    cot_all, inp_all, g_all, u_all, h_all, hg_all, gg_all, ug_all, val, slope_up, part,
    dw_v, gw_v, uw_v,
    ry_relay, ry_full, sy, sx, rx, q_own,
    ig_part, ig_core, ig_send, ig_recv, ig_red, ig_fin,
    lsem, ssem, rsem,
):
    row, col = lax.axis_index("row"), lax.axis_index("col")
    xh, y = lax.div(row, 4), lax.rem(row, 4)
    z, xl, co = lax.div(col, 4), lax.rem(lax.div(col, 2), 2), lax.rem(col, 2)
    y_next, y_prev, y_far = lax.rem(y + 1, 4), lax.rem(y + 3, 4), lax.rem(y + 2, 4)
    zs = [lax.rem(z + k, 8) for k in range(8)]
    hs = [1 - xl, xl]
    qs = [(1 - xl, 1 - co), (1 - xl, co), (xl, 1 - co), (xl, co)]

    yp = (xh * 4 + y_next, col)
    ym = (xh * 4 + y_prev, col)
    x2 = ((1 - xh) * 4 + y, col)
    mate = (row, col + 1 - 2 * co)
    side = (row, z * 4 + (1 - xl) * 2 + co)
    zd = [None] + [(row, zs[k] * 4 + xl * 2 + co) for k in range(1, 8)]
    near = (1, 7, 2, 6, 3, 5, 4)
    partners = [yp, ym, x2, mate, side] + zd[1:]

    def load(i, src, dst):
        cp = pltpu.make_async_copy(src, dst, lsem.at[i])
        cp.start()
        return cp

    sends = []

    def send(src, dst, device):
        i = len(sends)
        cp = pltpu.make_async_remote_copy(
            src_ref=src, dst_ref=dst, send_sem=ssem.at[i], recv_sem=rsem.at[i],
            device_id=device, device_id_type=MESH,
        )
        cp.start()
        sends.append(cp)
        return cp

    def to(ref, device):
        return send(ref, ref, device)

    def whole(ref):
        return lambda k, yy, half=None: ref.at[k, yy] if half is None else ref.at[k, yy, half]

    def chunk(ref, c):
        h, q = qs[c]

        def piece(k, yy, half=None):
            return ref.at[k, yy, h, q] if half is None else ref.at[k, yy, h, q, pl.ds(16 * half, 16)]

        return piece

    class AcrossFirst:
        def __init__(self, piece):
            self.piece = piece

        def start(self):
            own = self.piece(xh, y)
            self.across_cp = to(own, x2)
            self.up, self.down, self.rest = [to(own, yp)], [to(own, ym)], []

        def across(self):
            self.across_cp.wait_recv()
            other = self.piece(1 - xh, y)
            self.up.append(to(other, yp))
            self.down.append(to(other, ym))

        def relay(self, i):
            k = xh if i == 0 else 1 - xh
            self.up[i].wait_recv()
            self.rest.append(to(self.piece(k, y_prev, 0), yp))
            self.down[i].wait_recv()
            self.rest.append(to(self.piece(k, y_next, 1), ym))

        def done(self, i):
            for cp in self.rest[2 * i : 2 * i + 2]:
                cp.wait_recv()

    class AlongFirst:
        def __init__(self, piece):
            self.piece = piece

        def start_y(self):
            own = self.piece(xh, y)
            self.up, self.down = to(own, yp), to(own, ym)

        def start_x(self):
            self.x = [to(self.piece(xh, y), x2)]

        def near(self):
            self.up.wait_recv()
            self.x.append(to(self.piece(xh, y_prev), x2))
            self.down.wait_recv()
            self.x.append(to(self.piece(xh, y_next), x2))

        def relay(self):
            self.ru = to(self.piece(xh, y_prev, 0), yp)
            self.rd = to(self.piece(xh, y_next, 1), ym)

        def far(self):
            self.ru.wait_recv()
            self.rd.wait_recv()
            self.x.append(to(self.piece(xh, y_far), x2))

        def done(self):
            for cp in self.x:
                cp.wait_recv()

    class ColGather:
        def __init__(self, buf):
            self.buf = buf

        def start(self):
            self.side = to(self.buf.at[z, xl, co], side)

        def spread(self, c):
            if c == 0:
                self.side.wait_recv()
                self.cps = []
            self.cps.append([to(self.buf.at[z, hs[c], co], zd[k]) for k in near])

        def pair(self, c):
            for cp in self.cps[c]:
                cp.wait_recv()
            return to(self.buf.at[:, hs[c], co], mate)

    def act(k, yy):
        def step(i, carry):
            h, q = lax.div(i, 2), lax.rem(i, 2)
            gate_value = g_all[k, yy, h, q].astype(F32)
            up_value = u_all[k, yy, h, q].astype(F32)
            gelu_value, gelu_slope = gelu_parts(gate_value)
            h_all[k, yy, h, q] = (gelu_value * up_value).astype(BF16)
            val[k, yy, h, q] = gelu_value
            slope_up[k, yy, h, q] = up_value * gelu_slope
            return carry

        lax.fori_loop(0, 4, step, 0)

    def partial(c):
        h, q = qs[c]

        def tile(n, carry):
            cols = pl.ds(pl.multiple_of(n * NT, 128), NT)
            lhs = cot_all[:, h, q].reshape(256, W)
            part[c, :, :, :, cols] = dot_nn(lhs, dw_v[:, cols]).astype(BF16).reshape(2, 4, 32, NT)
            return carry

        lax.fori_loop(0, U // NT, tile, 0)

    lo, hi = pl.ds(0, 16), pl.ds(16, 16)

    class Scatter:
        def __init__(self, c):
            self.c = c

        def first(self):
            c = self.c
            self.relay_up = send(part.at[c, :, y_far, lo], ry_relay.at[c, 0], yp)
            self.relay_down = send(part.at[c, :, y_far, hi], ry_relay.at[c, 1], ym)
            direct_up = send(part.at[c, :, y_next, hi], ry_full.at[c, 0, :, hi], yp)
            direct_down = send(part.at[c, :, y_prev, lo], ry_full.at[c, 1, :, lo], ym)
            self.waits = [direct_up, direct_down]

        def second(self):
            c = self.c
            self.relay_up.wait_recv()
            sy[c, 0] = (part[c, :, y_next, 0:16].astype(F32) + ry_relay[c, 0].astype(F32)).astype(BF16)
            self.waits.append(send(sy.at[c, 0], ry_full.at[c, 0, :, lo], yp))
            self.relay_down.wait_recv()
            sy[c, 1] = (part[c, :, y_prev, 16:32].astype(F32) + ry_relay[c, 1].astype(F32)).astype(BF16)
            self.waits.append(send(sy.at[c, 1], ry_full.at[c, 1, :, hi], ym))

        def third(self):
            c = self.c
            for cp in self.waits:
                cp.wait_recv()

            def total(which):
                return (
                    part[c, which, y].astype(F32)
                    + ry_full[c, 0, which].astype(F32)
                    + ry_full[c, 1, which].astype(F32)
                )

            sx[c] = total(1 - xh).astype(BF16)
            self.across = send(sx.at[c], rx.at[c], x2)
            q_own[c] = total(xh)

        def last(self):
            c = self.c
            h, q = qs[c]
            self.across.wait_recv()
            hg_all[xh, y, h, q] = (q_own[c] + rx[c].astype(F32)).astype(BF16)

    def input_grad(c):
        h, q = qs[c]

        def step(i, carry):
            k, yy = lax.div(i, 4), lax.rem(i, 4)
            hidden_grad = hg_all[k, yy, h, q].astype(F32)
            gg_all[k, yy, h, q] = (hidden_grad * slope_up[k, yy, h, q]).astype(BF16)
            ug_all[k, yy, h, q] = (hidden_grad * val[k, yy, h, q]).astype(BF16)
            return carry

        lax.fori_loop(0, 8, step, 0)
        total = dot_nt(gg_all[:, :, h, q].reshape(256, U), gw_v[...])
        total += dot_nt(ug_all[:, :, h, q].reshape(256, U), uw_v[...])
        ig_part[c] = total.reshape(8, 32, W)

    def input_grad_mate(c):
        return send(ig_part.at[c], ig_core.at[c // 2], mate)

    def input_grad_spread(c, cp):
        cp.wait_recv()
        ig_send[c // 2] = (ig_part[c] + ig_core[c // 2]).astype(BF16)
        return [send(ig_send.at[c // 2, zs[k]], ig_recv.at[c // 2, k - 1], zd[k]) for k in near]

    def input_grad_sum(c, cps):
        total = ig_part[c, z] + ig_core[c // 2, z]
        for cp in cps:
            cp.wait_recv()
        for k in range(7):
            total += ig_recv[c // 2, k].astype(F32)
        ig_red[c // 2] = total

    def weight_grad(lhs_all, rhs_all, out):
        def tile(n, carry):
            cols = pl.ds(pl.multiple_of(n * NT, 128), NT)
            rhs = rhs_all[:, :, :, :, :, cols].reshape(1024, NT)
            out[:, cols] = dot_tn(lhs_all[...].reshape(1024, W), rhs).astype(BF16)
            return carry

        lax.fori_loop(0, U // NT, tile, 0)

    l_cot = load(0, cot_h, cot_all.at[z, xl, co])
    l_g = [load(9 + i, g_h.at[pl.ds(32 * i, 32)], g_all.at[xh, y, i // 2, i % 2]) for i in range(4)]
    l_u = [load(13 + i, u_h.at[pl.ds(32 * i, 32)], u_all.at[xh, y, i // 2, i % 2]) for i in range(4)]
    l_inp = load(1, inp_h, inp_all.at[z, xl, co])
    l_dw = load(2, dw_h, dw_v)
    l_gw = load(3, gw_h, gw_v)
    l_uw = load(4, uw_h, uw_v)

    barrier = pltpu.get_barrier_semaphore()
    for d in partners:
        pl.semaphore_signal(barrier, inc=1, device_id=d, device_id_type=MESH)
    for cp in [l_cot] + l_g + l_u + [l_inp]:
        cp.wait()
    with jax.named_scope("bar"):
        pl.semaphore_wait(barrier, len(partners))
    cot, inp = ColGather(cot_all), ColGather(inp_all)
    gate, up = AcrossFirst(whole(g_all)), AlongFirst(whole(u_all))
    rs = [Scatter(c) for c in range(4)]
    hg = [AlongFirst(chunk(hg_all, c)) for c in range(3)] + [AcrossFirst(chunk(hg_all, 3))]
    with jax.named_scope("start"):
        cot.start()
        gate.start()
        up.start_y()
        inp.start()
    with jax.named_scope("act"):
        act(xh, y)
    with jax.named_scope("cot0"):
        cot.spread(0)
        cot.spread(1)
    with jax.named_scope("upx"):
        up.start_x()
    with jax.named_scope("grelay"):
        gate.relay(0)
    with jax.named_scope("pair0"):
        m0 = cot.pair(0)
        l_dw.wait()
        m0.wait_recv()
    with jax.named_scope("p0"):
        partial(0)
        rs[0].first()
    with jax.named_scope("p1"):
        partial(1)
        rs[1].first()
    with jax.named_scope("upnear"):
        up.near()
    with jax.named_scope("B0"):
        rs[0].second()
    with jax.named_scope("pair1"):
        m1 = cot.pair(1)
        inp.spread(0)
        inp.spread(1)
        m1.wait_recv()
    with jax.named_scope("p2"):
        partial(2)
        rs[2].first()
    with jax.named_scope("B1"):
        rs[1].second()
    with jax.named_scope("act2"):
        act(xh, y_prev)
        act(xh, y_next)
    with jax.named_scope("C0"):
        rs[0].third()
    with jax.named_scope("p3"):
        partial(3)
        rs[3].first()
    with jax.named_scope("B2"):
        rs[2].second()
    with jax.named_scope("C1"):
        rs[1].third()
    with jax.named_scope("D0"):
        rs[0].last()
        hg[0].start_y()
        hg[0].start_x()
    with jax.named_scope("B3"):
        rs[3].second()
    with jax.named_scope("C2"):
        rs[2].third()
    with jax.named_scope("uprelay"):
        up.relay()
    with jax.named_scope("D1"):
        rs[1].last()
        hg[1].start_y()
        hg[1].start_x()
    with jax.named_scope("E0"):
        hg[0].near()
        hg[0].relay()
    with jax.named_scope("C3"):
        rs[3].third()
    with jax.named_scope("D2"):
        rs[2].last()
        hg[2].start_y()
        hg[2].start_x()
    with jax.named_scope("gacross"):
        gate.across()
    with jax.named_scope("F0"):
        hg[0].far()
    with jax.named_scope("E1"):
        hg[1].near()
        hg[1].relay()
    with jax.named_scope("upfar"):
        up.far()
        gate.done(0)
        act(xh, y_far)
    with jax.named_scope("D3"):
        rs[3].last()
        hg[3].start()
    with jax.named_scope("F1"):
        hg[1].far()
    with jax.named_scope("E2"):
        hg[2].near()
        hg[2].relay()
    with jax.named_scope("grelay1"):
        gate.relay(1)
    with jax.named_scope("R30"):
        hg[3].relay(0)
    with jax.named_scope("F2"):
        hg[2].far()
    with jax.named_scope("X3"):
        hg[3].across()
    with jax.named_scope("acts"):
        up.done()
        gate.done(1)
        for yy in range(4):
            act(1 - xh, yy)
    with jax.named_scope("ig0"):
        l_gw.wait()
        l_uw.wait()
        hg[0].done()
        input_grad(0)
        c0 = input_grad_mate(0)
    with jax.named_scope("R31"):
        hg[3].relay(1)
    with jax.named_scope("ig1"):
        hg[1].done()
        input_grad(1)
        z1 = input_grad_spread(1, c0)
    with jax.named_scope("ig2"):
        hg[2].done()
        input_grad(2)
        c2 = input_grad_mate(2)
    with jax.named_scope("hg3done"):
        hg[3].done(0)
        hg[3].done(1)
    with jax.named_scope("ig3"):
        input_grad(3)
        z3 = input_grad_spread(3, c2)
    with jax.named_scope("ig1sum"):
        input_grad_sum(1, z1)
        fin = send(ig_red.at[0], ig_fin, side)
    with jax.named_scope("dwg"):
        weight_grad(cot_all, h_all, dwg_o)
        outs = []
    with jax.named_scope("wg"):
        m2, m3 = inp.pair(0), inp.pair(1)
        m2.wait_recv()
        m3.wait_recv()
        weight_grad(inp_all, gg_all, gwg_o)
        weight_grad(inp_all, ug_all, uwg_o)
    with jax.named_scope("ig3sum"):
        input_grad_sum(3, z3)
    with jax.named_scope("fin"):
        fin.wait_recv()
        ig_o[...] = (ig_red[1] + ig_fin[...]).astype(BF16)
    with jax.named_scope("drain"):
        for cp in sends:
            cp.wait_send()
        for cp in outs:
            cp.wait()


def write_out(a, b, c, d, a_o, b_o, c_o, d_o, sems):
    cps = [pltpu.make_async_copy(s, o, sems.at[i]) for i, (s, o) in enumerate(((a, a_o), (b, b_o), (c, c_o), (d, d_o)))]
    for cp in cps:
        cp.start()
    for cp in cps:
        cp.wait()


def body(layer_inputs, cotangent, gate_saved, up_saved, gate_weight, up_weight, down_weight):
    any_spec = pl.BlockSpec(memory_space=pl.ANY)

    def bf(*shape):
        return pltpu.VMEM(shape, BF16)

    def f32(*shape):
        return pltpu.VMEM(shape, F32)

    input_grad, gate_grad, up_grad, down_grad = pl.pallas_call(
        kernel,
        out_shape=(
            bf(32, W),
            bf(W, U),
            bf(W, U),
            bf(W, U),
        ),
        in_specs=[any_spec] * 7,
        out_specs=[pl.BlockSpec(memory_space=pltpu.VMEM)] * 4,
        scratch_shapes=[
            bf(8, 2, 2, 32, W), bf(8, 2, 2, 32, W),
            *[bf(2, 4, 2, 2, 32, U) for _ in range(6)],
            f32(2, 4, 2, 2, 32, U), f32(2, 4, 2, 2, 32, U), bf(4, 2, 4, 32, U),
            bf(W, U), bf(W, U), bf(W, U),
            bf(4, 2, 2, 16, U), bf(4, 2, 2, 32, U), bf(4, 2, 2, 16, U), bf(4, 32, U), bf(4, 32, U), f32(4, 32, U),
            f32(4, 8, 32, W), f32(2, 8, 32, W), bf(2, 8, 32, W), bf(2, 7, 32, W), f32(2, 32, W), f32(32, W),
            pltpu.SemaphoreType.DMA((17,)),
            pltpu.SemaphoreType.DMA((N_REMOTE,)),
            pltpu.SemaphoreType.DMA((N_REMOTE,)),
        ],
        compiler_params=pltpu.CompilerParams(
            collective_id=0, has_side_effects=True, vmem_limit_bytes=56 * 2**20
        ),
        cost_estimate=pl.CostEstimate(flops=8 * 10**9, bytes_accessed=9 * 10**6, transcendentals=150000),
    )(layer_inputs, cotangent, gate_saved, up_saved, gate_weight, up_weight, down_weight.T)
    return input_grad, gate_grad, up_grad, down_grad.T


def solution(mesh):
    placed = (
        P("col", "row"),
        P("col", "row"),
        P("row", "col"),
        P("row", "col"),
        P("row", "col"),
        P("row", "col"),
        P("col", "row"),
    )
    return jax.shard_map(
        body,
        mesh=mesh,
        in_specs=placed,
        out_specs=(P("col", "row"), P("row", "col"), P("row", "col"), P("col", "row")),
        check_vma=False,
    )
```

```python
import functools

import jax
import jax.numpy as jnp
from jax import lax
from jax.experimental import pallas as pl
from jax.experimental.pallas import tpu as pltpu
from jax.sharding import PartitionSpec as P

SCALE_INNER = 0.7978845608028654
CUBIC_COEF = 0.044715
MESH = pl.DeviceIdType.MESH
BF16 = jnp.bfloat16
F32 = jnp.float32

W = 576
U = 1152
N_REMOTE = 140


def gelu_parts(gate_value):
    inner_term = SCALE_INNER * (gate_value + CUBIC_COEF * gate_value * gate_value * gate_value)
    tangent = jnp.tanh(inner_term)
    gelu_value = 0.5 * gate_value * (1.0 + tangent)
    gelu_slope = 0.5 * (1.0 + tangent) + 0.5 * gate_value * (
        1.0 - tangent * tangent
    ) * SCALE_INNER * (1.0 + 3.0 * CUBIC_COEF * gate_value * gate_value)
    return (gelu_value, gelu_slope)


def dot_nt(a, b):
    return lax.dot_general(a, b, (((1,), (1,)), ((), ())), preferred_element_type=F32)


def dot_nn(a, b):
    return lax.dot_general(a, b, (((1,), (0,)), ((), ())), preferred_element_type=F32)


def dot_tn(a, b):
    return lax.dot_general(a, b, (((0,), (0,)), ((), ())), preferred_element_type=F32)


def kernel(
    inp_h, cot_h, g_h, u_h, gw_h, uw_h, dw_h,
    ig_o, gwg_o, uwg_o, dwg_o,
    cot_all, inp_all, g_all, u_all, h_all, hg_all, gg_all, ug_all, val, slope_up, part, part32,
    dw_v, gw_v, uw_v,
    ry_relay, ry_full, sy, sx, rx, q_own,
    ig_part, ig_core, ig_send, ig_recv, ig_red, ig_fin,
    lsem, ssem, rsem,
):
    row, col = lax.axis_index("row"), lax.axis_index("col")
    xh, y = lax.div(row, 4), lax.rem(row, 4)
    z, xl, co = lax.div(col, 4), lax.rem(lax.div(col, 2), 2), lax.rem(col, 2)
    y_next, y_prev, y_far = lax.rem(y + 1, 4), lax.rem(y + 3, 4), lax.rem(y + 2, 4)
    zs = [lax.rem(z + k, 8) for k in range(8)]
    hs = [1 - xl, xl]
    qs = [(1 - xl, 1 - co), (1 - xl, co), (xl, 1 - co), (xl, co)]

    yp = (xh * 4 + y_next, col)
    ym = (xh * 4 + y_prev, col)
    x2 = ((1 - xh) * 4 + y, col)
    mate = (row, col + 1 - 2 * co)
    side = (row, z * 4 + (1 - xl) * 2 + co)
    zd = [None] + [(row, zs[k] * 4 + xl * 2 + co) for k in range(1, 8)]
    near = (1, 7, 2, 6, 3, 5, 4)
    partners = [yp, ym, x2, mate, side] + zd[1:]

    def load(i, src, dst):
        cp = pltpu.make_async_copy(src, dst, lsem.at[i])
        cp.start()
        return cp

    sends = []

    def send(src, dst, device, now=True):
        i = len(sends)
        cp = pltpu.make_async_remote_copy(
            src_ref=src, dst_ref=dst, send_sem=ssem.at[i], recv_sem=rsem.at[i],
            device_id=device, device_id_type=MESH,
        )
        if now:
            cp.start()
        sends.append(cp)
        return cp

    def to(ref, device):
        return send(ref, ref, device)

    def whole(ref):
        return lambda k, yy, half=None: ref.at[k, yy] if half is None else ref.at[k, yy, half]

    def chunk(ref, c):
        h, q = qs[c]

        def piece(k, yy, half=None):
            return ref.at[k, yy, h, q] if half is None else ref.at[k, yy, h, q, pl.ds(16 * half, 16)]

        return piece

    class AcrossFirst:
        def __init__(self, piece):
            self.piece = piece

        def start(self):
            own = self.piece(xh, y)
            self.across_cp = to(own, x2)
            self.up, self.down, self.rest = [to(own, yp)], [to(own, ym)], []

        def across(self):
            self.across_cp.wait_recv()
            other = self.piece(1 - xh, y)
            self.up.append(to(other, yp))
            self.down.append(to(other, ym))

        def relay(self, i):
            k = xh if i == 0 else 1 - xh
            self.up[i].wait_recv()
            self.rest.append(to(self.piece(k, y_prev, 0), yp))
            self.down[i].wait_recv()
            self.rest.append(to(self.piece(k, y_next, 1), ym))

        def done(self, i):
            for cp in self.rest[2 * i : 2 * i + 2]:
                cp.wait_recv()

    class AlongFirst:
        def __init__(self, piece):
            self.piece = piece

        def start_y(self):
            own = self.piece(xh, y)
            self.up, self.down = to(own, yp), to(own, ym)

        def start_x(self):
            self.x = [to(self.piece(xh, y), x2)]

        def near(self):
            self.up.wait_recv()
            self.x.append(to(self.piece(xh, y_prev), x2))
            self.down.wait_recv()
            self.x.append(to(self.piece(xh, y_next), x2))

        def relay(self):
            self.ru = to(self.piece(xh, y_prev, 0), yp)
            self.rd = to(self.piece(xh, y_next, 1), ym)

        def far(self):
            self.ru.wait_recv()
            self.rd.wait_recv()
            self.x.append(to(self.piece(xh, y_far), x2))

        def done(self):
            for cp in self.x:
                cp.wait_recv()

    class ColGather:
        def __init__(self, buf):
            self.buf = buf

        def start(self):
            self.side = to(self.buf.at[z, xl, co], side)

        def spread(self, c):
            if c == 0:
                self.side.wait_recv()
                self.cps = []
            self.cps.append([to(self.buf.at[z, hs[c], co], zd[k]) for k in near])

        def pair(self, c):
            for cp in self.cps[c]:
                cp.wait_recv()
            return to(self.buf.at[:, hs[c], co], mate)

    def act(k, yy):
        def step(i, carry):
            h, q = lax.div(i, 2), lax.rem(i, 2)
            gate_value = g_all[k, yy, h, q].astype(F32)
            up_value = u_all[k, yy, h, q].astype(F32)
            gelu_value, gelu_slope = gelu_parts(gate_value)
            h_all[k, yy, h, q] = (gelu_value * up_value).astype(BF16)
            val[k, yy, h, q] = gelu_value
            slope_up[k, yy, h, q] = up_value * gelu_slope
            return carry

        lax.fori_loop(0, 4, step, 0)

    def partial(c):
        h, q = qs[c]

        total = dot_nn(cot_all[:, h, q].reshape(256, W), dw_v[...]).reshape(2, 4, 32, U)
        part32[c] = total
        part[c] = total.astype(BF16)

    lo, hi = pl.ds(0, 16), pl.ds(16, 16)

    class Scatter:
        def __init__(self, c):
            self.c = c

        def first(self):
            c = self.c
            self.relay_up = send(part.at[c, :, y_far, lo], ry_relay.at[c, 0], yp)
            self.relay_down = send(part.at[c, :, y_far, hi], ry_relay.at[c, 1], ym)
            direct_up = send(part.at[c, :, y_next, hi], ry_full.at[c, 0, :, hi], yp)
            direct_down = send(part.at[c, :, y_prev, lo], ry_full.at[c, 1, :, lo], ym)
            self.waits = [direct_up, direct_down]

        def second(self):
            c = self.c
            self.relay_up.wait_recv()
            sy[c, 0] = (part32[c, :, y_next, 0:16] + ry_relay[c, 0].astype(F32)).astype(BF16)
            self.waits.append(send(sy.at[c, 0], ry_full.at[c, 0, :, lo], yp))
            self.relay_down.wait_recv()
            sy[c, 1] = (part32[c, :, y_prev, 16:32] + ry_relay[c, 1].astype(F32)).astype(BF16)
            self.waits.append(send(sy.at[c, 1], ry_full.at[c, 1, :, hi], ym))

        def third(self):
            c = self.c
            for cp in self.waits:
                cp.wait_recv()

            def total(which):
                return (
                    part32[c, which, y]
                    + ry_full[c, 0, which].astype(F32)
                    + ry_full[c, 1, which].astype(F32)
                )

            sx[c] = total(1 - xh).astype(BF16)
            self.across = send(sx.at[c], rx.at[c], x2)
            q_own[c] = total(xh)

        def last(self):
            c = self.c
            h, q = qs[c]
            self.across.wait_recv()
            hg_all[xh, y, h, q] = (q_own[c] + rx[c].astype(F32)).astype(BF16)

    def input_grad(cs, k):
        for c in cs:
            h, q = qs[c]

            def step(yy, carry, h=h, q=q):
                hidden_grad = hg_all[k, yy, h, q].astype(F32)
                gg_all[k, yy, h, q] = (hidden_grad * slope_up[k, yy, h, q]).astype(BF16)
                ug_all[k, yy, h, q] = (hidden_grad * val[k, yy, h, q]).astype(BF16)
                return carry

            lax.fori_loop(0, 4, step, 0)

        def rows(ref):
            return jnp.concatenate([ref[k, :, qs[c][0], qs[c][1]].reshape(128, U) for c in cs], axis=0)

        total = dot_nt(rows(gg_all), gw_v[...])
        total += dot_nt(rows(ug_all), uw_v[...])
        for i, c in enumerate(cs):
            ig_part[c, pl.ds(4 * k, 4)] = total[128 * i : 128 * i + 128].reshape(4, 32, W)

    def input_grad_add(c, k):
        at = pl.ds(4 * k, 4)
        ig_send[c // 2, at] = (ig_part[c, at] + ig_core[c // 2, at]).astype(BF16)

    def input_grad_copies(c):
        return [send(ig_send.at[c // 2, zs[k]], ig_recv.at[c // 2, k - 1], zd[k], now=False) for k in near]

    def spread_some(k, cps):
        for i, j in enumerate(near):

            @pl.when(lax.div(zs[j], 4) == k)
            def _(cp=cps[i]):
                cp.start()

    def input_grad_mate(c, k):
        at = pl.ds(4 * k, 4)
        return send(ig_part.at[c, at], ig_core.at[c // 2, at], mate)

    def input_grad_sum(c, cps):
        total = ig_part[c, z] + ig_core[c // 2, z]
        for cp in cps:
            cp.wait_recv()
        for k in range(7):
            total += ig_recv[c // 2, k].astype(F32)
        ig_red[c // 2] = total

    def weight_grad(lhs_all, rhs_all, out):
        out[...] = dot_tn(lhs_all[...].reshape(1024, W), rhs_all[...].reshape(1024, U)).astype(BF16)

    l_cot = load(0, cot_h, cot_all.at[z, xl, co])
    l_g = [load(9 + i, g_h.at[pl.ds(32 * i, 32)], g_all.at[xh, y, i // 2, i % 2]) for i in range(4)]
    l_u = [load(13 + i, u_h.at[pl.ds(32 * i, 32)], u_all.at[xh, y, i // 2, i % 2]) for i in range(4)]
    l_inp = load(1, inp_h, inp_all.at[z, xl, co])
    l_dw = load(2, dw_h, dw_v)
    l_gw = load(3, gw_h, gw_v)
    l_uw = load(4, uw_h, uw_v)

    barrier = pltpu.get_barrier_semaphore()
    for d in partners:
        pl.semaphore_signal(barrier, inc=1, device_id=d, device_id_type=MESH)
    for cp in [l_cot] + l_g + l_u + [l_inp]:
        cp.wait()
    with jax.named_scope("bar"):
        pl.semaphore_wait(barrier, len(partners))
    cot, inp = ColGather(cot_all), ColGather(inp_all)
    gate, up = AcrossFirst(whole(g_all)), AlongFirst(whole(u_all))
    rs = [Scatter(c) for c in range(4)]
    hg = [AlongFirst(chunk(hg_all, c)) for c in range(3)] + [AcrossFirst(chunk(hg_all, 3))]
    with jax.named_scope("start"):
        cot.start()
        gate.start()
        up.start_y()
        inp.start()
    with jax.named_scope("act"):
        act(xh, y)
    with jax.named_scope("cot0"):
        cot.spread(0)
        cot.spread(1)
    with jax.named_scope("upx"):
        up.start_x()
    with jax.named_scope("grelay"):
        gate.relay(0)
    with jax.named_scope("pair0"):
        m0 = cot.pair(0)
        l_dw.wait()
        m0.wait_recv()
    with jax.named_scope("p0"):
        partial(0)
        rs[0].first()
    with jax.named_scope("p1"):
        partial(1)
        rs[1].first()
    with jax.named_scope("upnear"):
        up.near()
    with jax.named_scope("B0"):
        rs[0].second()
    with jax.named_scope("pair1"):
        m1 = cot.pair(1)
        inp.spread(0)
        inp.spread(1)
        m1.wait_recv()
    with jax.named_scope("p2"):
        partial(2)
        rs[2].first()
    with jax.named_scope("B1"):
        rs[1].second()
    with jax.named_scope("act2"):
        act(xh, y_prev)
        act(xh, y_next)
    with jax.named_scope("C0"):
        rs[0].third()
    with jax.named_scope("p3"):
        partial(3)
        rs[3].first()
    with jax.named_scope("B2"):
        rs[2].second()
    with jax.named_scope("C1"):
        rs[1].third()
    with jax.named_scope("D0"):
        rs[0].last()
        hg[0].start_y()
        hg[0].start_x()
    with jax.named_scope("B3"):
        rs[3].second()
    with jax.named_scope("C2"):
        rs[2].third()
    with jax.named_scope("uprelay"):
        up.relay()
    with jax.named_scope("D1"):
        rs[1].last()
        hg[1].start_y()
        hg[1].start_x()
    with jax.named_scope("E0"):
        hg[0].near()
        hg[0].relay()
    with jax.named_scope("C3"):
        rs[3].third()
    with jax.named_scope("gacross"):
        gate.across()
    with jax.named_scope("D2"):
        rs[2].last()
        hg[2].start_y()
        hg[2].start_x()
    with jax.named_scope("F0"):
        hg[0].far()
    with jax.named_scope("E1"):
        hg[1].near()
        hg[1].relay()
    with jax.named_scope("upfar"):
        up.far()
        gate.done(0)
        act(xh, y_far)
    with jax.named_scope("D3"):
        rs[3].last()
        hg[3].start()
    with jax.named_scope("F1"):
        hg[1].far()
    with jax.named_scope("E2"):
        hg[2].near()
        hg[2].relay()
    with jax.named_scope("grelay1"):
        gate.relay(1)
    with jax.named_scope("R30"):
        hg[3].relay(0)
    with jax.named_scope("F2"):
        hg[2].far()
    with jax.named_scope("X3"):
        hg[3].across()
    with jax.named_scope("lw"):
        l_gw.wait()
        l_uw.wait()
    with jax.named_scope("igown"):
        input_grad([0, 1, 2], xh)
        m0a, m2a = input_grad_mate(0, xh), input_grad_mate(2, xh)
        z1 = input_grad_copies(1)
        m0a.wait_recv()
        input_grad_add(1, xh)
        spread_some(xh, z1)
    with jax.named_scope("R31"):
        hg[3].relay(1)
    with jax.named_scope("acts"):
        up.done()
        gate.done(1)
        for yy in range(4):
            act(1 - xh, yy)
    with jax.named_scope("igother"):
        for c in range(3):
            hg[c].done()
        input_grad([0, 1, 2], 1 - xh)
        m0b, m2b = input_grad_mate(0, 1 - xh), input_grad_mate(2, 1 - xh)
        m0b.wait_recv()
        input_grad_add(1, 1 - xh)
        spread_some(1 - xh, z1)
    with jax.named_scope("ig3own"):
        hg[3].done(0)
        input_grad([3], xh)
        m2a.wait_recv()
        z3 = input_grad_copies(3)
        input_grad_add(3, xh)
        spread_some(xh, z3)
    with jax.named_scope("ig3b"):
        hg[3].done(1)
        input_grad([3], 1 - xh)
        m2b.wait_recv()
        input_grad_add(3, 1 - xh)
        spread_some(1 - xh, z3)
    with jax.named_scope("ig1sum"):
        input_grad_sum(1, z1)
        fin = send(ig_red.at[0], ig_fin, side)
    with jax.named_scope("dwg"):
        weight_grad(cot_all, h_all, dwg_o)
        outs = []
    with jax.named_scope("wg"):
        m2, m3 = inp.pair(0), inp.pair(1)
        m2.wait_recv()
        m3.wait_recv()
        weight_grad(inp_all, gg_all, gwg_o)
        weight_grad(inp_all, ug_all, uwg_o)
    with jax.named_scope("ig3sum"):
        input_grad_sum(3, z3)
    with jax.named_scope("fin"):
        fin.wait_recv()
        ig_o[...] = (ig_red[1] + ig_fin[...]).astype(BF16)
    with jax.named_scope("drain"):
        for cp in sends:
            cp.wait_send()
        for cp in outs:
            cp.wait()


def write_out(a, b, c, d, a_o, b_o, c_o, d_o, sems):
    cps = [pltpu.make_async_copy(s, o, sems.at[i]) for i, (s, o) in enumerate(((a, a_o), (b, b_o), (c, c_o), (d, d_o)))]
    for cp in cps:
        cp.start()
    for cp in cps:
        cp.wait()


def body(layer_inputs, cotangent, gate_saved, up_saved, gate_weight, up_weight, down_weight):
    any_spec = pl.BlockSpec(memory_space=pl.ANY)

    def bf(*shape):
        return pltpu.VMEM(shape, BF16)

    def f32(*shape):
        return pltpu.VMEM(shape, F32)

    input_grad, gate_grad, up_grad, down_grad = pl.pallas_call(
        kernel,
        out_shape=(
            bf(32, W),
            bf(W, U),
            bf(W, U),
            bf(W, U),
        ),
        in_specs=[any_spec] * 7,
        out_specs=[pl.BlockSpec(memory_space=pltpu.VMEM)] * 4,
        scratch_shapes=[
            bf(8, 2, 2, 32, W), bf(8, 2, 2, 32, W),
            *[bf(2, 4, 2, 2, 32, U) for _ in range(6)],
            f32(2, 4, 2, 2, 32, U), f32(2, 4, 2, 2, 32, U), bf(4, 2, 4, 32, U), f32(4, 2, 4, 32, U),
            bf(W, U), bf(W, U), bf(W, U),
            bf(4, 2, 2, 16, U), bf(4, 2, 2, 32, U), bf(4, 2, 2, 16, U), bf(4, 32, U), bf(4, 32, U), f32(4, 32, U),
            f32(4, 8, 32, W), f32(2, 8, 32, W), bf(2, 8, 32, W), bf(2, 7, 32, W), f32(2, 32, W), f32(32, W),
            pltpu.SemaphoreType.DMA((17,)),
            pltpu.SemaphoreType.DMA((N_REMOTE,)),
            pltpu.SemaphoreType.DMA((N_REMOTE,)),
        ],
        compiler_params=pltpu.CompilerParams(
            collective_id=0, has_side_effects=True, vmem_limit_bytes=56 * 2**20
        ),
        cost_estimate=pl.CostEstimate(flops=8 * 10**9, bytes_accessed=9 * 10**6, transcendentals=150000),
    )(layer_inputs, cotangent, gate_saved, up_saved, gate_weight, up_weight, down_weight.T)
    return input_grad, gate_grad, up_grad, down_grad.T


def solution(mesh):
    placed = (
        P("col", "row"),
        P("col", "row"),
        P("row", "col"),
        P("row", "col"),
        P("row", "col"),
        P("row", "col"),
        P("col", "row"),
    )
    return jax.shard_map(
        body,
        mesh=mesh,
        in_specs=placed,
        out_specs=(P("col", "row"), P("row", "col"), P("row", "col"), P("col", "row")),
        check_vma=False,
    )
```

```python
import functools

import jax
import jax.numpy as jnp
from jax import lax
from jax.experimental import pallas as pl
from jax.experimental.pallas import tpu as pltpu
from jax.sharding import PartitionSpec as P

SCALE_INNER = 0.7978845608028654
CUBIC_COEF = 0.044715
MESH = pl.DeviceIdType.MESH
BF16 = jnp.bfloat16
F32 = jnp.float32

W = 576
U = 1152
N_REMOTE = 140


def gelu_parts(gate_value):
    inner_term = SCALE_INNER * (gate_value + CUBIC_COEF * gate_value * gate_value * gate_value)
    tangent = jnp.tanh(inner_term)
    gelu_value = 0.5 * gate_value * (1.0 + tangent)
    gelu_slope = 0.5 * (1.0 + tangent) + 0.5 * gate_value * (
        1.0 - tangent * tangent
    ) * SCALE_INNER * (1.0 + 3.0 * CUBIC_COEF * gate_value * gate_value)
    return (gelu_value, gelu_slope)


def dot_nt(a, b):
    return lax.dot_general(a, b, (((1,), (1,)), ((), ())), preferred_element_type=F32)


def dot_nn(a, b):
    return lax.dot_general(a, b, (((1,), (0,)), ((), ())), preferred_element_type=F32)


def dot_tn(a, b):
    return lax.dot_general(a, b, (((0,), (0,)), ((), ())), preferred_element_type=F32)


def kernel(
    inp_h, cot_h, g_h, u_h, gw_h, uw_h, dw_h,
    ig_o, gwg_o, uwg_o, dwg_o,
    cot_all, inp_all, g_all, u_all, h_all, hg_all, gg_all, ug_all, val, slope_up, part, part32,
    dw_v, gw_v, uw_v,
    ry_relay, ry_full, sy, sx, rx, q_own,
    ig_part, ig_core, ig_send, ig_recv, ig_red, ig_fin,
    lsem, ssem, rsem,
):
    row, col = lax.axis_index("row"), lax.axis_index("col")
    xh, y = lax.div(row, 4), lax.rem(row, 4)
    z, xl, co = lax.div(col, 4), lax.rem(lax.div(col, 2), 2), lax.rem(col, 2)
    y_next, y_prev, y_far = lax.rem(y + 1, 4), lax.rem(y + 3, 4), lax.rem(y + 2, 4)
    zs = [lax.rem(z + k, 8) for k in range(8)]
    hs = [1 - xl, xl]
    qs = [(1 - xl, 1 - co), (1 - xl, co), (xl, 1 - co), (xl, co)]

    yp = (xh * 4 + y_next, col)
    ym = (xh * 4 + y_prev, col)
    x2 = ((1 - xh) * 4 + y, col)
    mate = (row, col + 1 - 2 * co)
    side = (row, z * 4 + (1 - xl) * 2 + co)
    zd = [None] + [(row, zs[k] * 4 + xl * 2 + co) for k in range(1, 8)]
    near = (1, 7, 2, 6, 3, 5, 4)
    partners = [yp, ym, x2, mate, side] + zd[1:]

    def load(i, src, dst):
        cp = pltpu.make_async_copy(src, dst, lsem.at[i])
        cp.start()
        return cp

    sends = []

    def send(src, dst, device, now=True):
        i = len(sends)
        cp = pltpu.make_async_remote_copy(
            src_ref=src, dst_ref=dst, send_sem=ssem.at[i], recv_sem=rsem.at[i],
            device_id=device, device_id_type=MESH,
        )
        if now:
            cp.start()
        sends.append(cp)
        return cp

    def to(ref, device):
        return send(ref, ref, device)

    def whole(ref):
        return lambda k, yy, half=None: ref.at[k, yy] if half is None else ref.at[k, yy, half]

    def chunk(ref, c):
        h, q = qs[c]

        def piece(k, yy, half=None):
            return ref.at[k, yy, h, q] if half is None else ref.at[k, yy, h, q, pl.ds(16 * half, 16)]

        return piece

    class AcrossFirst:
        def __init__(self, piece):
            self.piece = piece

        def start(self):
            own = self.piece(xh, y)
            self.across_cp = to(own, x2)
            self.up, self.down, self.rest = [to(own, yp)], [to(own, ym)], []

        def across(self):
            self.across_cp.wait_recv()
            other = self.piece(1 - xh, y)
            self.up.append(to(other, yp))
            self.down.append(to(other, ym))

        def relay(self, i):
            k = xh if i == 0 else 1 - xh
            self.up[i].wait_recv()
            self.rest.append(to(self.piece(k, y_prev, 0), yp))
            self.down[i].wait_recv()
            self.rest.append(to(self.piece(k, y_next, 1), ym))

        def done(self, i):
            for cp in self.rest[2 * i : 2 * i + 2]:
                cp.wait_recv()

    class AlongFirst:
        def __init__(self, piece):
            self.piece = piece

        def start_y(self):
            own = self.piece(xh, y)
            self.up, self.down = to(own, yp), to(own, ym)

        def start_x(self):
            self.x = [to(self.piece(xh, y), x2)]

        def near(self):
            self.up.wait_recv()
            self.x.append(to(self.piece(xh, y_prev), x2))
            self.down.wait_recv()
            self.x.append(to(self.piece(xh, y_next), x2))

        def relay(self):
            self.ru = to(self.piece(xh, y_prev, 0), yp)
            self.rd = to(self.piece(xh, y_next, 1), ym)

        def far(self):
            self.ru.wait_recv()
            self.rd.wait_recv()
            self.x.append(to(self.piece(xh, y_far), x2))

        def done(self):
            for cp in self.x:
                cp.wait_recv()

    class ColGather:
        def __init__(self, buf):
            self.buf = buf

        def start(self):
            self.side = to(self.buf.at[z, xl, co], side)

        def spread(self, c):
            if c == 0:
                self.side.wait_recv()
                self.cps = []
            self.cps.append([to(self.buf.at[z, hs[c], co], zd[k]) for k in near])

        def pair(self, c):
            for cp in self.cps[c]:
                cp.wait_recv()
            return to(self.buf.at[:, hs[c], co], mate)

    def act(k, yy):
        def step(i, carry):
            h, q = lax.div(i, 2), lax.rem(i, 2)
            gate_value = g_all[k, yy, h, q].astype(F32)
            up_value = u_all[k, yy, h, q].astype(F32)
            gelu_value, gelu_slope = gelu_parts(gate_value)
            h_all[k, yy, h, q] = (gelu_value * up_value).astype(BF16)
            val[k, yy, h, q] = gelu_value
            slope_up[k, yy, h, q] = up_value * gelu_slope
            return carry

        lax.fori_loop(0, 4, step, 0)

    def partial(c):
        h, q = qs[c]

        total = dot_nn(cot_all[:, h, q].reshape(256, W), dw_v[...]).reshape(2, 4, 32, U)
        part32[c] = total
        part[c] = total.astype(BF16)

    lo, hi = pl.ds(0, 16), pl.ds(16, 16)

    class Scatter:
        def __init__(self, c):
            self.c = c

        def first(self):
            c = self.c
            self.relay_up = send(part.at[c, :, y_far, lo], ry_relay.at[c, 0], yp)
            self.relay_down = send(part.at[c, :, y_far, hi], ry_relay.at[c, 1], ym)
            direct_up = send(part.at[c, :, y_next, hi], ry_full.at[c, 0, :, hi], yp)
            direct_down = send(part.at[c, :, y_prev, lo], ry_full.at[c, 1, :, lo], ym)
            self.waits = [direct_up, direct_down]

        def second(self):
            c = self.c
            self.relay_up.wait_recv()
            sy[c, 0] = (part32[c, :, y_next, 0:16] + ry_relay[c, 0].astype(F32)).astype(BF16)
            self.waits.append(send(sy.at[c, 0], ry_full.at[c, 0, :, lo], yp))
            self.relay_down.wait_recv()
            sy[c, 1] = (part32[c, :, y_prev, 16:32] + ry_relay[c, 1].astype(F32)).astype(BF16)
            self.waits.append(send(sy.at[c, 1], ry_full.at[c, 1, :, hi], ym))

        def third(self):
            c = self.c
            for cp in self.waits:
                cp.wait_recv()

            def total(which):
                return (
                    part32[c, which, y]
                    + ry_full[c, 0, which].astype(F32)
                    + ry_full[c, 1, which].astype(F32)
                )

            sx[c] = total(1 - xh).astype(BF16)
            self.across = send(sx.at[c], rx.at[c], x2)
            q_own[c] = total(xh)

        def last(self):
            c = self.c
            h, q = qs[c]
            self.across.wait_recv()
            hg_all[xh, y, h, q] = (q_own[c] + rx[c].astype(F32)).astype(BF16)

    def input_grad(cs, k):
        for c in cs:
            h, q = qs[c]

            def step(yy, carry, h=h, q=q):
                hidden_grad = hg_all[k, yy, h, q].astype(F32)
                gg_all[k, yy, h, q] = (hidden_grad * slope_up[k, yy, h, q]).astype(BF16)
                ug_all[k, yy, h, q] = (hidden_grad * val[k, yy, h, q]).astype(BF16)
                return carry

            lax.fori_loop(0, 4, step, 0)

        def rows(ref):
            return jnp.concatenate([ref[k, :, qs[c][0], qs[c][1]].reshape(128, U) for c in cs], axis=0)

        total = dot_nt(rows(gg_all), gw_v[...])
        total += dot_nt(rows(ug_all), uw_v[...])
        for i, c in enumerate(cs):
            ig_part[c, pl.ds(4 * k, 4)] = total[128 * i : 128 * i + 128].reshape(4, 32, W)

    def input_grad_add(c, k):
        at = pl.ds(4 * k, 4)
        ig_send[c // 2, at] = (ig_part[c, at] + ig_core[c // 2, at]).astype(BF16)

    def input_grad_copies(c):
        return [send(ig_send.at[c // 2, zs[k]], ig_recv.at[c // 2, k - 1], zd[k], now=False) for k in near]

    def spread_some(k, cps):
        for i, j in enumerate(near):

            @pl.when(lax.div(zs[j], 4) == k)
            def _(cp=cps[i]):
                cp.start()

    def input_grad_mate(c, k):
        at = pl.ds(4 * k, 4)
        return send(ig_part.at[c, at], ig_core.at[c // 2, at], mate)

    def input_grad_sum(c, cps):
        total = ig_part[c, z] + ig_core[c // 2, z]
        for cp in cps:
            cp.wait_recv()
        for k in range(7):
            total += ig_recv[c // 2, k].astype(F32)
        ig_red[c // 2] = total

    def weight_grad(lhs_all, rhs_all, out):
        out[...] = dot_tn(lhs_all[...].reshape(1024, W), rhs_all[...].reshape(1024, U)).astype(BF16)

    l_cot = load(0, cot_h, cot_all.at[z, xl, co])
    l_g = [load(9 + i, g_h.at[pl.ds(32 * i, 32)], g_all.at[xh, y, i // 2, i % 2]) for i in range(4)]
    l_u = [load(13 + i, u_h.at[pl.ds(32 * i, 32)], u_all.at[xh, y, i // 2, i % 2]) for i in range(4)]
    l_inp = load(1, inp_h, inp_all.at[z, xl, co])
    l_dw = load(2, dw_h, dw_v)
    l_gw = load(3, gw_h, gw_v)
    l_uw = load(4, uw_h, uw_v)

    barrier = pltpu.get_barrier_semaphore()
    for d in partners:
        pl.semaphore_signal(barrier, inc=1, device_id=d, device_id_type=MESH)
    for cp in [l_cot] + l_g + l_u + [l_inp]:
        cp.wait()
    with jax.named_scope("bar"):
        pl.semaphore_wait(barrier, len(partners))
    cot, inp = ColGather(cot_all), ColGather(inp_all)
    gate, up = AcrossFirst(whole(g_all)), AlongFirst(whole(u_all))
    rs = [Scatter(c) for c in range(4)]
    hg = [AlongFirst(chunk(hg_all, c)) for c in range(3)] + [AcrossFirst(chunk(hg_all, 3))]
    with jax.named_scope("start"):
        cot.start()
        gate.start()
        up.start_y()
        inp.start()
    with jax.named_scope("act"):
        act(xh, y)
    with jax.named_scope("cot0"):
        cot.spread(0)
        cot.spread(1)
    with jax.named_scope("upx"):
        up.start_x()
    with jax.named_scope("grelay"):
        gate.relay(0)
    with jax.named_scope("pair0"):
        m0 = cot.pair(0)
        l_dw.wait()
        m0.wait_recv()
    with jax.named_scope("p0"):
        partial(0)
        rs[0].first()
    with jax.named_scope("p1"):
        partial(1)
        rs[1].first()
    with jax.named_scope("upnear"):
        up.near()
    with jax.named_scope("B0"):
        rs[0].second()
    with jax.named_scope("pair1"):
        m1 = cot.pair(1)
        inp.spread(0)
        inp.spread(1)
        m1.wait_recv()
    with jax.named_scope("p2"):
        partial(2)
        rs[2].first()
    with jax.named_scope("B1"):
        rs[1].second()
    with jax.named_scope("act2"):
        act(xh, y_prev)
        act(xh, y_next)
    with jax.named_scope("C0"):
        rs[0].third()
    with jax.named_scope("p3"):
        partial(3)
        rs[3].first()
    with jax.named_scope("B2"):
        rs[2].second()
    with jax.named_scope("C1"):
        rs[1].third()
    with jax.named_scope("D0"):
        rs[0].last()
        hg[0].start_y()
        hg[0].start_x()
    with jax.named_scope("B3"):
        rs[3].second()
    with jax.named_scope("C2"):
        rs[2].third()
    with jax.named_scope("uprelay"):
        up.relay()
    with jax.named_scope("D1"):
        rs[1].last()
        hg[1].start_y()
        hg[1].start_x()
    with jax.named_scope("E0"):
        hg[0].near()
        hg[0].relay()
    with jax.named_scope("C3"):
        rs[3].third()
    with jax.named_scope("gacross"):
        gate.across()
    with jax.named_scope("D2"):
        rs[2].last()
        hg[2].start_y()
        hg[2].start_x()
    with jax.named_scope("F0"):
        hg[0].far()
    with jax.named_scope("upfar"):
        up.far()
        gate.done(0)
        act(xh, y_far)
    with jax.named_scope("E1"):
        hg[1].near()
        hg[1].relay()
    with jax.named_scope("D3"):
        rs[3].last()
        hg[3].start()
    with jax.named_scope("F1"):
        hg[1].far()
    with jax.named_scope("E2"):
        hg[2].near()
        hg[2].relay()
    with jax.named_scope("grelay1"):
        gate.relay(1)
    with jax.named_scope("R30"):
        hg[3].relay(0)
    with jax.named_scope("F2"):
        hg[2].far()
    with jax.named_scope("X3"):
        hg[3].across()
    with jax.named_scope("lw"):
        l_gw.wait()
        l_uw.wait()
    with jax.named_scope("igown"):
        input_grad([0, 1, 2], xh)
        m0a, m2a = input_grad_mate(0, xh), input_grad_mate(2, xh)
        z1 = input_grad_copies(1)
        m0a.wait_recv()
        input_grad_add(1, xh)
        spread_some(xh, z1)
    with jax.named_scope("R31"):
        hg[3].relay(1)
    with jax.named_scope("acts"):
        up.done()
        gate.done(1)
        for yy in range(4):
            act(1 - xh, yy)
    with jax.named_scope("igother"):
        for c in range(3):
            hg[c].done()
        input_grad([0, 1, 2], 1 - xh)
        m0b, m2b = input_grad_mate(0, 1 - xh), input_grad_mate(2, 1 - xh)
        m0b.wait_recv()
        input_grad_add(1, 1 - xh)
        spread_some(1 - xh, z1)
    with jax.named_scope("ig3own"):
        hg[3].done(0)
        input_grad([3], xh)
        m2a.wait_recv()
        z3 = input_grad_copies(3)
        input_grad_add(3, xh)
        spread_some(xh, z3)
    with jax.named_scope("ig3b"):
        hg[3].done(1)
        input_grad([3], 1 - xh)
        m2b.wait_recv()
        input_grad_add(3, 1 - xh)
        spread_some(1 - xh, z3)
    with jax.named_scope("dwg"):
        weight_grad(cot_all, h_all, dwg_o)
        outs = []
    with jax.named_scope("gate_wg"):
        m2, m3 = inp.pair(0), inp.pair(1)
        m2.wait_recv()
        m3.wait_recv()
        weight_grad(inp_all, gg_all, gwg_o)
    with jax.named_scope("ig1sum"):
        input_grad_sum(1, z1)
        fin = send(ig_red.at[0], ig_fin, side)
    with jax.named_scope("up_wg"):
        weight_grad(inp_all, ug_all, uwg_o)
    with jax.named_scope("ig3sum"):
        input_grad_sum(3, z3)
    with jax.named_scope("fin"):
        fin.wait_recv()
        ig_o[...] = (ig_red[1] + ig_fin[...]).astype(BF16)
    with jax.named_scope("drain"):
        for cp in sends:
            cp.wait_send()
        for cp in outs:
            cp.wait()


def write_out(a, b, c, d, a_o, b_o, c_o, d_o, sems):
    cps = [pltpu.make_async_copy(s, o, sems.at[i]) for i, (s, o) in enumerate(((a, a_o), (b, b_o), (c, c_o), (d, d_o)))]
    for cp in cps:
        cp.start()
    for cp in cps:
        cp.wait()


def body(layer_inputs, cotangent, gate_saved, up_saved, gate_weight, up_weight, down_weight):
    any_spec = pl.BlockSpec(memory_space=pl.ANY)

    def bf(*shape):
        return pltpu.VMEM(shape, BF16)

    def f32(*shape):
        return pltpu.VMEM(shape, F32)

    input_grad, gate_grad, up_grad, down_grad = pl.pallas_call(
        kernel,
        out_shape=(
            bf(32, W),
            bf(W, U),
            bf(W, U),
            bf(W, U),
        ),
        in_specs=[any_spec] * 7,
        out_specs=[pl.BlockSpec(memory_space=pltpu.VMEM)] * 4,
        scratch_shapes=[
            bf(8, 2, 2, 32, W), bf(8, 2, 2, 32, W),
            *[bf(2, 4, 2, 2, 32, U) for _ in range(6)],
            f32(2, 4, 2, 2, 32, U), f32(2, 4, 2, 2, 32, U), bf(4, 2, 4, 32, U), f32(4, 2, 4, 32, U),
            bf(W, U), bf(W, U), bf(W, U),
            bf(4, 2, 2, 16, U), bf(4, 2, 2, 32, U), bf(4, 2, 2, 16, U), bf(4, 32, U), bf(4, 32, U), f32(4, 32, U),
            f32(4, 8, 32, W), f32(2, 8, 32, W), bf(2, 8, 32, W), bf(2, 7, 32, W), f32(2, 32, W), f32(32, W),
            pltpu.SemaphoreType.DMA((17,)),
            pltpu.SemaphoreType.DMA((N_REMOTE,)),
            pltpu.SemaphoreType.DMA((N_REMOTE,)),
        ],
        compiler_params=pltpu.CompilerParams(
            collective_id=0, has_side_effects=True, vmem_limit_bytes=56 * 2**20
        ),
        cost_estimate=pl.CostEstimate(flops=8 * 10**9, bytes_accessed=9 * 10**6, transcendentals=150000),
    )(layer_inputs, cotangent, gate_saved, up_saved, gate_weight, up_weight, down_weight.T)
    return input_grad, gate_grad, up_grad, down_grad.T


def solution(mesh):
    placed = (
        P("col", "row"),
        P("col", "row"),
        P("row", "col"),
        P("row", "col"),
        P("row", "col"),
        P("row", "col"),
        P("col", "row"),
    )
    return jax.shard_map(
        body,
        mesh=mesh,
        in_specs=placed,
        out_specs=(P("col", "row"), P("row", "col"), P("row", "col"), P("col", "row")),
        check_vma=False,
    )
```
